256 devices in a mesh: pipe: 16 (over y, z_hi), tensor: 16 (over x, z_lo, core).
Axes of the slice: x: 4, y: 4, z: 8 (z_hi: 4, z_lo: 2; z = z_hi * 2 + z_lo), core: 2. Of those that a mesh axis runs over, the one named last changes fastest.
Arguments:
- hidden: bfloat16 [256, 12288], P('pipe', 'tensor'), may hold values from -9 to 9
- targets: int32 [256], P('pipe'), may hold values from 0 to 65535
- weight: bfloat16 [65536, 12288], P('pipe', 'tensor'), may hold values from -1 to 1
Outputs:
- losses: float32 [256], P('pipe')
- hidden_grad: bfloat16 [256, 12288], P('pipe', 'tensor')
- weight_grad: bfloat16 [65536, 12288], P('pipe', 'tensor')
The draws below stay inside these ranges and needn't reach their ends.
All inputs are finite; a program needn't handle non-finite values.
Results may differ from the reference program's by a relative error of at most 0.0039.
Values may be sent and summed in bfloat16 or wider, within the bound.
No kernel may reach another device: no remote copies, remote signals or barrier semaphores. Data moves between devices by JAX's collectives and lax.ppermute only.
A program may use at most 64 MiB of HBM per device.

```python
import math
import jax
import jax.numpy as jnp
from jax import lax

D = 12288
VOCAB_SECTION = 4096
TOKENS = 256
VOCAB = 65536


def base_rows(key, rows):
    row_base = jax.random.fold_in(key, 104)

    def one_row(index):
        return jax.random.normal(jax.random.fold_in(row_base, index), (D,), jnp.float32)
    return jax.vmap(one_row)(rows) * (3.0 / math.sqrt(D))


def draw_weight(key, part):
    values = base_rows(key, jnp.arange(VOCAB, dtype=jnp.int32))
    return jnp.clip(values, -1.0, 1.0).astype(jnp.bfloat16)


def draw_hidden(key, part):
    owned = jax.random.fold_in(key, 2)
    values = jax.random.normal(owned, (TOKENS, D), jnp.float32)
    return jnp.clip(values, -9.0, 9.0).astype(jnp.bfloat16)


def touch_ends(entries, key, least, top_value):
    longest = entries.shape.index(max(entries.shape))
    spots = []
    for shift in (0, 1):
        where = [jax.random.randint(jax.random.fold_in(key, axis), (), 0, length) for axis, length in enumerate(entries.shape)]
        where[longest] = (where[longest] + shift) % entries.shape[longest]
        spots.append(tuple(where))
    return entries.at[spots[0]].set(least).at[spots[1]].set(top_value)


def setup_inputs(seed: int = 0) -> dict:
    seeds = jax.random.split(jax.random.key(seed), 4)
    hidden = draw_hidden(jax.random.fold_in(seeds[3], 71), 0)
    targets = touch_ends(jax.random.randint(seeds[1], (TOKENS,), 0, VOCAB), jax.random.fold_in(seeds[1], 1), 0, VOCAB - 1).astype(jnp.int32)
    weight = draw_weight(jax.random.fold_in(seeds[3], 71), 0)
    return {"hidden": hidden, "targets": targets, "weight": weight}


def reference(hidden, targets, weight):
    logits = lax.dot_general(hidden, weight, (((1,), (1,)), ((), ())), preferred_element_type=jnp.float32)
    top = lax.optimization_barrier(jnp.max(logits, axis=1))
    shifted = jnp.exp(logits - top[:, None])
    total = lax.optimization_barrier(jnp.sum(shifted, axis=1))
    columns = jnp.arange(VOCAB, dtype=jnp.int32)
    onehot = (columns[None, :] == targets[:, None]).astype(jnp.float32)
    picked = lax.optimization_barrier(jnp.sum(logits * onehot, axis=1))
    losses = top + jnp.log(total) - picked
    grad_logits = (4.0 * (shifted / total[:, None] - onehot)).astype(jnp.bfloat16)
    hidden_grad = jnp.dot(grad_logits, weight, preferred_element_type=jnp.float32).astype(jnp.bfloat16)
    blocks = grad_logits.T.reshape(VOCAB // VOCAB_SECTION, VOCAB_SECTION, TOKENS)

    def block_grad(block):
        return jnp.dot(block, hidden, preferred_element_type=jnp.float32).astype(jnp.bfloat16)
    weight_grad = lax.map(block_grad, blocks).reshape(VOCAB, D)
    return (losses, hidden_grad, weight_grad)
```

```python
import jax
import jax.numpy as jnp
from jax import lax
from jax.sharding import Mesh, PartitionSpec as P

PIPE = ("y", "zh")
CHIPS = ("x", "zl")
TENSOR = ("x", "zl", "core")
SWAP = [(0, 1), (1, 0)]


def split3(v):
    a = v.astype(jnp.bfloat16)
    r = v - lax.reduce_precision(v, 8, 7)
    b = r.astype(jnp.bfloat16)
    r = r - lax.reduce_precision(r, 8, 7)
    return jnp.stack([a, b, r.astype(jnp.bfloat16)], axis=-1)


def join3(v):
    v = v.astype(jnp.float32)
    return v[..., 0] + v[..., 1] + v[..., 2]


def spread(v, axes, n):
    return lax.all_to_all(jnp.broadcast_to(v[None], (n,) + v.shape), axes, 0, 0)


def shards(hidden, targets, weight):
    rows, width = hidden.shape
    vocab = weight.shape[0]
    half = vocab // 2
    section = lax.axis_index(PIPE)
    core = lax.axis_index("core")
    chip = lax.axis_index(CHIPS)

    ids = jnp.stack([targets // 256, targets % 256], axis=1).astype(jnp.bfloat16)
    packed = jnp.concatenate([hidden, jnp.pad(ids, ((0, 0), (0, 126)))], axis=1)
    gathered = spread(packed, PIPE, 16).reshape(16 * rows, width + 128)
    tokens = gathered.shape[0]
    per_chip = tokens // 8
    full = gathered[:, :width]
    ids = gathered[:, width : width + 2].astype(jnp.int32)
    all_targets = ids[:, 0] * 256 + ids[:, 1]

    w_own = lax.dynamic_slice_in_dim(weight, core * half, half, 0)
    w_oth = lax.dynamic_slice_in_dim(weight, (1 - core) * half, half, 0)
    dims = (((1,), (1,)), ((), ()))
    send = lax.dot_general(full, w_oth, dims, preferred_element_type=jnp.float32)
    got = lax.ppermute(send.astype(jnp.float16), "core", SWAP)
    keep = lax.dot_general(full, w_own, dims, preferred_element_type=jnp.float32)
    keep = (keep + got.astype(jnp.float32)).astype(jnp.float16)
    parts = lax.all_to_all(keep.reshape(8, per_chip, half), CHIPS, 0, 0)
    logits = jnp.sum(parts.astype(jnp.float32), axis=0)

    mine = lax.dynamic_slice_in_dim(all_targets, chip * per_chip, per_chip, 0)
    columns = section * vocab + core * half + jnp.arange(half, dtype=jnp.int32)
    top = jnp.max(logits, axis=1)
    e = jnp.exp(logits - top[:, None])
    s = jnp.sum(e, axis=1)
    pick = jnp.sum(jnp.where(columns[None, :] == mine[:, None], logits, 0.0), axis=1)
    stats = jnp.concatenate([split3(top), split3(s), split3(pick)], axis=1)
    block = jnp.concatenate([e.astype(jnp.bfloat16), jnp.pad(stats, ((0, 0), (0, 119)))], axis=1)
    own = spread(block, CHIPS, 8).reshape(tokens, half + 128)
    oth = lax.ppermute(own, "core", SWAP)

    def unpack(b):
        st = b[:, half : half + 9].reshape(tokens, 3, 3)
        return join3(st)

    st_own, st_oth = unpack(own), unpack(oth)
    all_stats = jnp.concatenate([st_own.T, st_oth.T, jnp.zeros((2, tokens), jnp.float32)], axis=0)
    everyone = spread(all_stats, PIPE, 16)
    upper = jnp.maximum(jnp.max(everyone[:, 0], axis=0), jnp.max(everyone[:, 3], axis=0))
    total = jnp.sum(
        everyone[:, 1] * jnp.exp(everyone[:, 0] - upper) + everyone[:, 4] * jnp.exp(everyone[:, 3] - upper), axis=0
    )
    picked = jnp.sum(everyone[:, 2] + everyone[:, 5], axis=0)
    every_loss = upper + jnp.log(total) - picked
    losses = lax.dynamic_slice_in_dim(every_loss, section * rows, rows, 0)

    def grad(b, st, which):
        scale = jnp.exp(st[:, 0] - upper) / total
        columns = section * vocab + which * half + jnp.arange(half, dtype=jnp.int32)
        onehot = (columns[None, :] == all_targets[:, None]).astype(jnp.float32)
        return (4.0 * (b[:, :half].astype(jnp.float32) * scale[:, None] - onehot)).astype(jnp.bfloat16)

    g_own, g_oth = grad(own, st_own, core), grad(oth, st_oth, 1 - core)
    hg = jnp.dot(g_own, w_own, preferred_element_type=jnp.float32)
    hg = hg + jnp.dot(g_oth, w_oth, preferred_element_type=jnp.float32)
    sent = (hg * 4096.0).astype(jnp.float16).reshape(16, rows, width)
    parts = lax.all_to_all(sent, PIPE, 0, 0)
    hidden_grad = (jnp.sum(parts.astype(jnp.float32), axis=0) * (1.0 / 4096.0)).astype(jnp.bfloat16)

    g_full = jnp.where(
        core == 0, jnp.concatenate([g_own, g_oth], axis=1), jnp.concatenate([g_oth, g_own], axis=1)
    )
    weight_grad = lax.dot_general(
        g_full, full, (((0,), (0,)), ((), ())), preferred_element_type=jnp.float32
    ).astype(jnp.bfloat16)
    return (losses, hidden_grad, weight_grad)


def solution(mesh):
    fine = Mesh(mesh.devices.reshape(4, 4, 4, 2, 2), PIPE + TENSOR)
    return jax.shard_map(
        shards,
        mesh=fine,
        in_specs=(P(PIPE, TENSOR), P(PIPE), P(PIPE, TENSOR)),
        out_specs=(P(PIPE), P(PIPE, TENSOR), P(PIPE, TENSOR)),
        check_vma=False,
    )
```

```python
import functools

import jax
import jax.numpy as jnp
from jax import lax
from jax.experimental import pallas as pl
from jax.experimental.pallas import tpu as pltpu
from jax.sharding import Mesh, PartitionSpec as P

PIPE = ("y", "zh")
CHIPS = ("x", "zl")
TENSOR = ("x", "zl", "core")
SWAP = [(0, 1), (1, 0)]
TILE = 512


def join3(v, k):
    return v[3 * k : 3 * k + 1] + v[3 * k + 1 : 3 * k + 2] + v[3 * k + 2 : 3 * k + 3]


def decode(ids):
    ids = ids.astype(jnp.float32).astype(jnp.int32)
    return ids[:, 0:1] * 256 + ids[:, 1:2]


def spread(v, axes, n):
    return lax.all_to_all(jnp.broadcast_to(v[None], (n,) + v.shape), axes, 0, 0)


def far(v):
    return pltpu.with_memory_space_constraint(v, pltpu.HBM)


def params(mib):
    return pltpu.CompilerParams(vmem_limit_bytes=mib << 20)


def pack_kernel(targets, hidden_ref, out_ref):
    rows, width = hidden_ref.shape
    row = lax.broadcasted_iota(jnp.int32, (rows, 128), 0)
    lane = lax.broadcasted_iota(jnp.int32, (rows, 128), 1)
    ids = jnp.zeros((rows, 128), jnp.int32)
    for r in range(rows):
        t = targets[r]
        high = lax.shift_right_logical(t, 8)
        low = t - high * 256
        ids = jnp.where((row == r) & (lane == 0), high, ids)
        ids = jnp.where((row == r) & (lane == 1), low, ids)
    ids = ids.astype(jnp.float32).astype(jnp.bfloat16)
    for d in range(out_ref.shape[0]):
        out_ref[d, :, :width] = hidden_ref[...]
        out_ref[d, :, width:] = ids


def pack(hidden, targets, copies):
    rows, width = hidden.shape
    return pl.pallas_call(
        pack_kernel,
        in_specs=[pl.BlockSpec(memory_space=pltpu.SMEM), pl.BlockSpec(memory_space=pltpu.VMEM)],
        out_specs=pl.BlockSpec(memory_space=pltpu.VMEM),
        out_shape=jax.ShapeDtypeStruct((copies, rows, width + 128), jnp.bfloat16),
        compiler_params=params(60),
    )(targets, hidden)


def softmax_kernel(place, logits_ref, ids_ref, picks_ref, out_ref):
    rows, half = logits_ref.shape
    logits = logits_ref[...]
    top = jnp.max(logits, axis=1, keepdims=True)
    e = jnp.exp(logits - top)
    s = jnp.sum(e, axis=1, keepdims=True)
    columns = lax.broadcasted_iota(jnp.int32, logits.shape, 1) + place[1]
    pick = jnp.sum(jnp.where(columns == decode(ids_ref[...]), logits, 0.0), axis=1, keepdims=True)
    lane = lax.broadcasted_iota(jnp.int32, (rows, 128), 1)
    stats = jnp.zeros((rows, 128), jnp.float32)
    for k, v in enumerate((top, s, pick)):
        for part in range(3):
            rounded = v.astype(jnp.bfloat16).astype(jnp.float32)
            stats = jnp.where(lane == 3 * k + part, rounded, stats)
            v = v - rounded
    e, stats = e.astype(jnp.bfloat16), stats.astype(jnp.bfloat16)
    for d in range(out_ref.shape[0]):
        out_ref[d, :, :half] = e
        out_ref[d, :, half:] = stats


def softmax(place, logits, gathered, picks, copies):
    rows, half = logits.shape
    last = gathered.shape[1] // 128 - 1
    return pl.pallas_call(
        softmax_kernel,
        grid_spec=pltpu.PrefetchScalarGridSpec(
            num_scalar_prefetch=1,
            grid=(1,),
            in_specs=[
                pl.BlockSpec((rows, half), lambda i, s: (0, 0)),
                pl.BlockSpec((rows, 128), lambda i, s: (s[0], last)),
                pl.BlockSpec(memory_space=pltpu.HBM),
            ],
            out_specs=pl.BlockSpec((copies, rows, half + 128), lambda i, s: (0, 0, 0)),
        ),
        out_shape=jax.ShapeDtypeStruct((copies, rows, half + 128), jnp.bfloat16),
        compiler_params=params(8),
    )(place, logits, gathered, far(picks))


def rows_kernel(block_ref, out_ref):
    v = block_ref[...].astype(jnp.float32).T
    out_ref[...] = jnp.concatenate([join3(v, 0), join3(v, 1), join3(v, 2), v[16:21]], axis=0)


def stat_rows(own):
    tokens, width = own.shape
    return pl.pallas_call(
        rows_kernel,
        grid=(1,),
        in_specs=[pl.BlockSpec((tokens, 128), lambda i: (0, width // 128 - 1))],
        out_specs=pl.BlockSpec((8, tokens), lambda i: (0, 0)),
        out_shape=jax.ShapeDtypeStruct((8, tokens), jnp.float32),
        compiler_params=params(4),
    )(own)


def join_kernel(own_ref, oth_ref, out_ref):
    both = jnp.concatenate([own_ref[0:3], oth_ref[0:3], own_ref[6:8]], axis=0)
    for d in range(out_ref.shape[0]):
        out_ref[d] = both


def join_stats(own, oth, copies):
    return pl.pallas_call(
        join_kernel,
        out_shape=jax.ShapeDtypeStruct((copies,) + own.shape, jnp.float32),
        compiler_params=params(4),
    )(own, oth)


def scale_kernel(every_ref, own_ref, oth_ref, u_ref, scale_ref, loss_ref):
    every = every_ref[...]
    upper = jnp.max(jnp.maximum(every[:, 0], every[:, 3]), axis=0, keepdims=True)
    total = jnp.sum(
        every[:, 1] * jnp.exp(every[:, 0] - upper) + every[:, 4] * jnp.exp(every[:, 3] - upper), axis=0, keepdims=True
    )
    picked = jnp.sum(every[:, 2] + every[:, 5], axis=0, keepdims=True)
    loss_ref[...] = upper + jnp.log(total) - picked
    a = jnp.exp(own_ref[0:1] - upper) / total
    b = jnp.exp(oth_ref[0:1] - upper) / total
    scale_ref[...] = jnp.concatenate([a, b, jnp.zeros((126, a.shape[1]), jnp.float32)], axis=0).T


def scale_columns(everyone, own, oth, u):
    tokens = own.shape[1]
    return pl.pallas_call(
        scale_kernel,
        in_specs=[pl.BlockSpec(memory_space=pltpu.VMEM)] * 3 + [pl.BlockSpec(memory_space=pl.ANY)],
        out_shape=[
            jax.ShapeDtypeStruct((tokens, 128), jnp.float32),
            jax.ShapeDtypeStruct((1, tokens), jnp.float32),
        ],
        compiler_params=params(4),
    )(everyone, own, oth, u)


def row_blocks(place, w_ref, held, sems):
    step = held.shape[0] // sems.shape[0]
    copies = []
    for slot in range(sems.shape[0]):
        which, k = divmod(slot, sems.shape[0] // 2)
        source = pl.ds(pl.multiple_of(place[which], step) + k * step, step)
        copies.append(
            pltpu.make_async_copy(w_ref.at[source], held.at[pl.ds(slot * step, step)], sems.at[slot])
        )
    return step, copies


def picks_kernel(place, ids_ref, w_ref, t_ref, held, sems):
    step, copies = row_blocks(place, w_ref, held, sems)
    for copy in copies:
        copy.start()
    target = decode(ids_ref[...]) - place[2]
    t = None
    for slot, copy in enumerate(copies):
        columns = lax.broadcasted_iota(jnp.int32, (target.shape[0], step), 1) + slot * step
        onehot = jnp.where(columns == target, 1.0, 0.0).astype(jnp.bfloat16)
        copy.wait()
        d = jnp.dot(onehot, held[slot * step : (slot + 1) * step], preferred_element_type=jnp.float32)
        t = d if t is None else t + d
    t_ref[...] = t.astype(jnp.bfloat16)


def picks_of(place, gathered, weight, tokens):
    width = weight.shape[1]
    last = gathered.shape[1] // 128 - 1
    return pl.pallas_call(
        picks_kernel,
        grid_spec=pltpu.PrefetchScalarGridSpec(
            num_scalar_prefetch=1,
            grid=(1,),
            in_specs=[
                pl.BlockSpec((tokens, 128), lambda i, s: (0, last)),
                pl.BlockSpec(memory_space=pltpu.HBM),
            ],
            out_specs=pl.BlockSpec((tokens, width), lambda i, s: (0, 0)),
            scratch_shapes=[pltpu.VMEM(weight.shape, weight.dtype), pltpu.SemaphoreType.DMA((4,))],
        ),
        out_shape=pltpu.HBM((tokens, width), jnp.bfloat16),
        compiler_params=params(24),
        cost_estimate=pl.CostEstimate(
            flops=2 * tokens * weight.size, bytes_accessed=2 * weight.size, transcendentals=0
        ),
    )(place, gathered, far(weight))


def product_kernel(place, own_ref, oth_ref, w_ref, u_ref, held, other, sems, sem):
    half = held.shape[0] // 2
    step, copies = row_blocks(place, w_ref, held, sems)
    fetch = pltpu.make_async_copy(oth_ref, other, sem)
    copies[0].start()
    copies[1].start()
    fetch.start()
    per_half = len(copies) // 2
    for which, p_ref in enumerate((own_ref, other)):
        u = None
        for k in range(per_half):
            slot = which * per_half + k
            copies[slot].wait()
            if slot + 2 < len(copies):
                copies[slot + 2].start()
            if slot == per_half:
                fetch.wait()
            d = jnp.dot(
                p_ref[:, k * step : (k + 1) * step],
                held[slot * step : (slot + 1) * step],
                preferred_element_type=jnp.float32,
            )
            u = d if u is None else u + d
        u_ref[which] = u


def products(place, own, oth, weight):
    tokens, width = own.shape[0], weight.shape[1]
    return pl.pallas_call(
        product_kernel,
        grid_spec=pltpu.PrefetchScalarGridSpec(
            num_scalar_prefetch=1,
            grid=(1,),
            in_specs=[
                pl.BlockSpec(own.shape, lambda i, s: (0, 0)),
                pl.BlockSpec(memory_space=pltpu.HBM),
                pl.BlockSpec(memory_space=pltpu.HBM),
            ],
            out_specs=pl.BlockSpec((2, tokens, width), lambda i, s: (0, 0, 0)),
            scratch_shapes=[
                pltpu.VMEM(weight.shape, weight.dtype),
                pltpu.VMEM(oth.shape, oth.dtype),
                pltpu.SemaphoreType.DMA((4,)),
                pltpu.SemaphoreType.DMA,
            ],
        ),
        out_shape=jax.ShapeDtypeStruct((2, tokens, width), jnp.float32),
        compiler_params=params(24),
        cost_estimate=pl.CostEstimate(
            flops=2 * tokens * weight.size, bytes_accessed=2 * weight.size, transcendentals=0
        ),
    )(place, own, far(oth), far(weight))


def weight_grad_kernel(steps, place, own_ref, oth_ref, hidden_ref, ids_ref, scale_ref, out_ref):
    i = pl.program_id(0)

    def tile(p_ref, which, j):
        columns = lax.broadcasted_iota(jnp.int32, p_ref.shape, 1) + (place[1 + which] + j * TILE)
        onehot = (columns == decode(ids_ref[...])).astype(jnp.float32)
        scale = scale_ref[:, which : which + 1]
        g = (4.0 * (p_ref[...].astype(jnp.float32) * scale - onehot)).astype(jnp.bfloat16)
        out_ref[...] = lax.dot_general(
            g, hidden_ref[...], (((0,), (0,)), ((), ())), preferred_element_type=jnp.float32
        ).astype(jnp.bfloat16)

    @pl.when(i < steps)
    def _():
        tile(own_ref, 0, i)

    @pl.when(i >= steps)
    def _():
        tile(oth_ref, 1, i - steps)


def weight_gradient(place, own, oth, gathered, scales, half, width):
    tokens = own.shape[0]
    last = gathered.shape[1] // 128 - 1
    steps = half // TILE
    return pl.pallas_call(
        functools.partial(weight_grad_kernel, steps),
        grid_spec=pltpu.PrefetchScalarGridSpec(
            num_scalar_prefetch=1,
            grid=(2 * steps,),
            in_specs=[
                pl.BlockSpec((tokens, TILE), lambda i, s: (0, jnp.minimum(i, steps - 1))),
                pl.BlockSpec((tokens, TILE), lambda i, s: (0, jnp.maximum(i - steps, 0))),
                pl.BlockSpec((tokens, width), lambda i, s: (0, 0)),
                pl.BlockSpec((tokens, 128), lambda i, s: (0, last)),
                pl.BlockSpec((tokens, 128), lambda i, s: (0, 0)),
            ],
            out_specs=pl.BlockSpec(
                (TILE, width), lambda i, s: (lax.rem(i + s[0] * steps, 2 * steps), 0)
            ),
        ),
        out_shape=jax.ShapeDtypeStruct((2 * half, width), jnp.bfloat16),
        compiler_params=pltpu.CompilerParams(vmem_limit_bytes=24 << 20),
        cost_estimate=pl.CostEstimate(
            flops=4 * tokens * half * width, bytes_accessed=4 * half * (width + tokens), transcendentals=0
        ),
    )(place, own, far(oth), gathered, gathered, scales)


def shards(hidden, targets, weight):
    rows, width = hidden.shape
    vocab = weight.shape[0]
    half = vocab // 2
    section = lax.axis_index(PIPE)
    core = lax.axis_index("core")
    chip = lax.axis_index(CHIPS)
    base_own = section * vocab + core * half
    base_oth = section * vocab + (1 - core) * half

    gathered = lax.all_to_all(pack(hidden, targets, 16), PIPE, 0, 0).reshape(16 * rows, width + 128)
    tokens = gathered.shape[0]
    per_chip = tokens // 8
    full = gathered[:, :width]

    w_own = lax.dynamic_slice_in_dim(weight, core * half, half, 0)
    w_oth = lax.dynamic_slice_in_dim(weight, (1 - core) * half, half, 0)
    dims = (((1,), (1,)), ((), ()))
    send = lax.dot_general(full, w_oth, dims, preferred_element_type=jnp.float32)
    got = lax.ppermute(send.astype(jnp.float16), "core", SWAP)
    keep = lax.dot_general(full, w_own, dims, preferred_element_type=jnp.float32)
    keep = lax.optimization_barrier(keep)
    keep = (keep + got.astype(jnp.float32)).astype(jnp.float16)
    parts = lax.all_to_all(keep.reshape(8, per_chip, half), CHIPS, 0, 0)
    logits = jnp.sum(parts.astype(jnp.float32), axis=0)
    picks = picks_of(jnp.stack([0, half, section * vocab]), gathered, weight, tokens)

    block = softmax(jnp.stack([chip, base_own]), logits, gathered, picks, 8)
    own = lax.all_to_all(block, CHIPS, 0, 0).reshape(tokens, half + 128)
    st_own = stat_rows(own)
    st_oth = lax.ppermute(st_own, "core", SWAP)
    own, st_oth = lax.optimization_barrier((own, st_oth))
    oth = lax.ppermute(own, "core", SWAP)
    everyone = lax.all_to_all(join_stats(st_own, st_oth, 16), PIPE, 0, 0)

    u = products(jnp.stack([core * half, (1 - core) * half]), own, oth, weight)

    scales, every_loss = scale_columns(everyone, st_own, st_oth, u)
    hg = scales[:, 0:1] * u[0] + scales[:, 1:2] * u[1] - picks.astype(jnp.float32)
    sent = (hg * 16384.0).astype(jnp.float16).reshape(16, rows, width)
    parts = lax.all_to_all(sent, PIPE, 0, 0)
    hidden_grad = (jnp.sum(parts.astype(jnp.float32), axis=0) * (1.0 / 4096.0)).astype(jnp.bfloat16)

    losses = lax.dynamic_slice_in_dim(every_loss[0], section * rows, rows, 0)
    weight_grad = weight_gradient(
        jnp.stack([core, base_own, base_oth]), own, oth, gathered, scales, half, width
    )
    return (losses, hidden_grad, weight_grad)


def solution(mesh):
    fine = Mesh(mesh.devices.reshape(4, 4, 4, 2, 2), PIPE + TENSOR)
    return jax.shard_map(
        shards,
        mesh=fine,
        in_specs=(P(PIPE, TENSOR), P(PIPE), P(PIPE, TENSOR)),
        out_specs=(P(PIPE), P(PIPE, TENSOR), P(PIPE, TENSOR)),
        check_vma=False,
    )
```

```python
import functools

import jax
import jax.numpy as jnp
from jax import lax
from jax.experimental import pallas as pl
from jax.experimental.pallas import tpu as pltpu
from jax.sharding import Mesh, PartitionSpec as P

PIPE = ("y", "zh")
CHIPS = ("x", "zl")
TENSOR = ("x", "zl", "core")
SWAP = [(0, 1), (1, 0)]
STEPS = [(1, 0), (3, 0), (0, 1), (2, 1), (2, 0), (1, 1), (3, 1)]
TILE = 512


def join3(v, k):
    return v[3 * k : 3 * k + 1] + v[3 * k + 1 : 3 * k + 2] + v[3 * k + 2 : 3 * k + 3]


def decode(ids):
    ids = ids.astype(jnp.float32).astype(jnp.int32)
    return ids[:, 0:1] * 256 + ids[:, 1:2]


def spread(v, axes, n):
    return lax.all_to_all(jnp.broadcast_to(v[None], (n,) + v.shape), axes, 0, 0)


def to_chip(v, step):
    dx, dz = step
    pairs = [(2 * x + z, 2 * ((x + dx) % 4) + (z ^ dz)) for x in range(4) for z in range(2)]
    return lax.ppermute(v, CHIPS, pairs)


def far(v):
    return pltpu.with_memory_space_constraint(v, pltpu.HBM)


def params(mib):
    return pltpu.CompilerParams(vmem_limit_bytes=mib << 20)


def pack_kernel(targets, hidden_ref, out_ref):
    rows, width = hidden_ref.shape
    row = lax.broadcasted_iota(jnp.int32, (rows, 128), 0)
    lane = lax.broadcasted_iota(jnp.int32, (rows, 128), 1)
    ids = jnp.zeros((rows, 128), jnp.int32)
    for r in range(rows):
        t = targets[r]
        high = lax.shift_right_logical(t, 8)
        low = t - high * 256
        ids = jnp.where((row == r) & (lane == 0), high, ids)
        ids = jnp.where((row == r) & (lane == 1), low, ids)
    ids = ids.astype(jnp.float32).astype(jnp.bfloat16)
    for d in range(out_ref.shape[0]):
        out_ref[d, :, :width] = hidden_ref[...]
        out_ref[d, :, width:] = ids


def pack(hidden, targets, copies):
    rows, width = hidden.shape
    return pl.pallas_call(
        pack_kernel,
        in_specs=[pl.BlockSpec(memory_space=pltpu.SMEM), pl.BlockSpec(memory_space=pltpu.VMEM)],
        out_specs=pl.BlockSpec(memory_space=pltpu.VMEM),
        out_shape=jax.ShapeDtypeStruct((copies, rows, width + 128), jnp.bfloat16),
        compiler_params=params(60),
    )(targets, hidden)


def softmax_kernel(place, logits_ref, ids_ref, out_ref):
    rows, half = logits_ref.shape
    logits = logits_ref[...]
    top = jnp.max(logits, axis=1, keepdims=True)
    e = jnp.exp(logits - top)
    s = jnp.sum(e, axis=1, keepdims=True)
    columns = lax.broadcasted_iota(jnp.int32, logits.shape, 1) + place[1]
    pick = jnp.sum(jnp.where(columns == decode(ids_ref[...]), logits, 0.0), axis=1, keepdims=True)
    lane = lax.broadcasted_iota(jnp.int32, (rows, 128), 1)
    stats = jnp.zeros((rows, 128), jnp.float32)
    for k, v in enumerate((top, s, pick)):
        for part in range(3):
            rounded = v.astype(jnp.bfloat16).astype(jnp.float32)
            stats = jnp.where(lane == 3 * k + part, rounded, stats)
            v = v - rounded
    out_ref[:, :half] = e.astype(jnp.bfloat16)
    out_ref[:, half:] = stats.astype(jnp.bfloat16)


def softmax(place, logits, ids):
    rows, half = logits.shape
    return pl.pallas_call(
        softmax_kernel,
        grid_spec=pltpu.PrefetchScalarGridSpec(
            num_scalar_prefetch=1,
            grid=(1,),
            in_specs=[
                pl.BlockSpec((rows, half), lambda i, s: (0, 0)),
                pl.BlockSpec((rows, 128), lambda i, s: (s[0], 0)),
            ],
            out_specs=pl.BlockSpec((rows, half + 128), lambda i, s: (0, 0)),
        ),
        out_shape=jax.ShapeDtypeStruct((rows, half + 128), jnp.bfloat16),
        compiler_params=params(8),
    )(place, logits, ids)


def assemble_kernel(place, *refs):
    blocks, (out_ref, stat_ref) = refs[:-2], refs[-2:]
    rows = blocks[0].shape[0]
    for r, block in enumerate(blocks):
        out_ref[pl.ds(pl.multiple_of(place[r] * rows, rows), rows)] = block[...]
    v = out_ref[:, out_ref.shape[1] - 128 :].astype(jnp.float32).T
    stat_ref[...] = jnp.concatenate([join3(v, 0), join3(v, 1), join3(v, 2), v[16:21]], axis=0)


def assemble(place, blocks):
    rows, width = blocks[0].shape
    tokens = rows * len(blocks)
    return pl.pallas_call(
        assemble_kernel,
        grid_spec=pltpu.PrefetchScalarGridSpec(
            num_scalar_prefetch=1,
            grid=(1,),
            in_specs=[pl.BlockSpec((rows, width), lambda i, s: (0, 0))] * len(blocks),
            out_specs=[
                pl.BlockSpec((tokens, width), lambda i, s: (0, 0)),
                pl.BlockSpec((8, tokens), lambda i, s: (0, 0)),
            ],
        ),
        out_shape=[
            jax.ShapeDtypeStruct((tokens, width), jnp.bfloat16),
            jax.ShapeDtypeStruct((8, tokens), jnp.float32),
        ],
        compiler_params=params(12),
    )(place, *blocks)


def join_kernel(own_ref, oth_ref, out_ref):
    both = jnp.concatenate([own_ref[0:3], oth_ref[0:3], own_ref[6:8]], axis=0)
    for d in range(out_ref.shape[0]):
        out_ref[d] = both


def join_stats(own, oth, copies):
    return pl.pallas_call(
        join_kernel,
        out_shape=jax.ShapeDtypeStruct((copies,) + own.shape, jnp.float32),
        compiler_params=params(4),
    )(own, oth)


def scale_kernel(every_ref, own_ref, oth_ref, u_ref, scale_ref, loss_ref):
    every = every_ref[...]
    upper = jnp.max(jnp.maximum(every[:, 0], every[:, 3]), axis=0, keepdims=True)
    total = jnp.sum(
        every[:, 1] * jnp.exp(every[:, 0] - upper) + every[:, 4] * jnp.exp(every[:, 3] - upper), axis=0, keepdims=True
    )
    picked = jnp.sum(every[:, 2] + every[:, 5], axis=0, keepdims=True)
    loss_ref[...] = upper + jnp.log(total) - picked
    a = jnp.exp(own_ref[0:1] - upper) / total
    b = jnp.exp(oth_ref[0:1] - upper) / total
    scale_ref[...] = jnp.concatenate([a, b, jnp.zeros((126, a.shape[1]), jnp.float32)], axis=0).T


def scale_columns(everyone, own, oth, u):
    tokens = own.shape[1]
    return pl.pallas_call(
        scale_kernel,
        in_specs=[pl.BlockSpec(memory_space=pltpu.VMEM)] * 3 + [pl.BlockSpec(memory_space=pl.ANY)],
        out_shape=[
            jax.ShapeDtypeStruct((tokens, 128), jnp.float32),
            jax.ShapeDtypeStruct((1, tokens), jnp.float32),
        ],
        compiler_params=params(4),
    )(everyone, own, oth, u)


def row_blocks(place, w_ref, held, sems):
    step = held.shape[0] // sems.shape[0]
    copies = []
    for slot in range(sems.shape[0]):
        which, k = divmod(slot, sems.shape[0] // 2)
        source = pl.ds(pl.multiple_of(place[which], step) + k * step, step)
        copies.append(
            pltpu.make_async_copy(w_ref.at[source], held.at[pl.ds(slot * step, step)], sems.at[slot])
        )
    return step, copies


def product_kernel(place, own_ref, ids_ref, oth_ref, w_ref, u_ref, t_ref, held, other, sems, sem):
    step, copies = row_blocks(place, w_ref, held, sems)
    fetch = pltpu.make_async_copy(oth_ref, other, sem)
    copies[0].start()
    copies[1].start()
    fetch.start()
    per_half = len(copies) // 2
    target = decode(ids_ref[...])
    tokens = target.shape[0]
    t = None
    for which, p_ref in enumerate((own_ref, other)):
        u = None
        for k in range(per_half):
            slot = which * per_half + k
            if slot == per_half:
                fetch.wait()
            columns = lax.broadcasted_iota(jnp.int32, (tokens, step), 1) + (place[2] + place[which] + k * step)
            onehot = jnp.where(columns == target, 1.0, 0.0).astype(jnp.bfloat16)
            both = jnp.concatenate([p_ref[:, k * step : (k + 1) * step], onehot], axis=0)
            copies[slot].wait()
            if slot + 2 < len(copies):
                copies[slot + 2].start()
            d = jnp.dot(both, held[slot * step : (slot + 1) * step], preferred_element_type=jnp.float32)
            u = d[:tokens] if u is None else u + d[:tokens]
            t = d[tokens:] if t is None else t + d[tokens:]
        u_ref[which] = u
    t_ref[...] = t.astype(jnp.bfloat16)


def products(place, own, oth, ids, weight):
    tokens, width = own.shape[0], weight.shape[1]
    return pl.pallas_call(
        product_kernel,
        grid_spec=pltpu.PrefetchScalarGridSpec(
            num_scalar_prefetch=1,
            grid=(1,),
            in_specs=[
                pl.BlockSpec(own.shape, lambda i, s: (0, 0)),
                pl.BlockSpec(ids.shape, lambda i, s: (0, 0)),
                pl.BlockSpec(memory_space=pltpu.HBM),
                pl.BlockSpec(memory_space=pltpu.HBM),
            ],
            out_specs=[
                pl.BlockSpec((2, tokens, width), lambda i, s: (0, 0, 0)),
                pl.BlockSpec((tokens, width), lambda i, s: (0, 0)),
            ],
            scratch_shapes=[
                pltpu.VMEM(weight.shape, weight.dtype),
                pltpu.VMEM(oth.shape, oth.dtype),
                pltpu.SemaphoreType.DMA((4,)),
                pltpu.SemaphoreType.DMA,
            ],
        ),
        out_shape=[
            jax.ShapeDtypeStruct((2, tokens, width), jnp.float32),
            jax.ShapeDtypeStruct((tokens, width), jnp.bfloat16),
        ],
        compiler_params=params(28),
        cost_estimate=pl.CostEstimate(
            flops=4 * tokens * weight.size, bytes_accessed=2 * weight.size, transcendentals=0
        ),
    )(place, own, ids, far(oth), far(weight))


def weight_grad_kernel(steps, place, own_ref, oth_ref, hidden_ref, ids_ref, scale_ref, out_ref):
    i = pl.program_id(0)

    def tile(p_ref, which, j):
        columns = lax.broadcasted_iota(jnp.int32, p_ref.shape, 1) + (place[1 + which] + j * TILE)
        onehot = (columns == decode(ids_ref[...])).astype(jnp.float32)
        scale = scale_ref[:, which : which + 1]
        g = (4.0 * (p_ref[...].astype(jnp.float32) * scale - onehot)).astype(jnp.bfloat16)
        out_ref[...] = lax.dot_general(
            g, hidden_ref[...], (((0,), (0,)), ((), ())), preferred_element_type=jnp.float32
        ).astype(jnp.bfloat16)

    @pl.when(i < steps)
    def _():
        tile(own_ref, 0, i)

    @pl.when(i >= steps)
    def _():
        tile(oth_ref, 1, i - steps)


def weight_gradient(place, own, oth, gathered, ids, scales, half, width):
    tokens = own.shape[0]
    steps = half // TILE
    return pl.pallas_call(
        functools.partial(weight_grad_kernel, steps),
        grid_spec=pltpu.PrefetchScalarGridSpec(
            num_scalar_prefetch=1,
            grid=(2 * steps,),
            in_specs=[
                pl.BlockSpec((tokens, TILE), lambda i, s: (0, jnp.minimum(i, steps - 1))),
                pl.BlockSpec((tokens, TILE), lambda i, s: (0, jnp.maximum(i - steps, 0))),
                pl.BlockSpec((tokens, width), lambda i, s: (0, 0)),
                pl.BlockSpec((tokens, 128), lambda i, s: (0, 0)),
                pl.BlockSpec((tokens, 128), lambda i, s: (0, 0)),
            ],
            out_specs=pl.BlockSpec(
                (TILE, width), lambda i, s: (lax.rem(i + s[0] * steps, 2 * steps), 0)
            ),
        ),
        out_shape=jax.ShapeDtypeStruct((2 * half, width), jnp.bfloat16),
        compiler_params=pltpu.CompilerParams(vmem_limit_bytes=24 << 20),
        cost_estimate=pl.CostEstimate(
            flops=4 * tokens * half * width, bytes_accessed=4 * half * (width + tokens), transcendentals=0
        ),
    )(place, own, far(oth), far(gathered), ids, scales)


def shards(hidden, targets, weight):
    rows, width = hidden.shape
    vocab = weight.shape[0]
    half = vocab // 2
    section = lax.axis_index(PIPE)
    core = lax.axis_index("core")
    chip = lax.axis_index(CHIPS)
    base_own = section * vocab + core * half
    base_oth = section * vocab + (1 - core) * half

    gathered = lax.all_to_all(pack(hidden, targets, 16), PIPE, 0, 0).reshape(16 * rows, width + 128)
    tokens = gathered.shape[0]
    per_chip = tokens // 8
    full, ids = gathered[:, :width], gathered[:, width:]

    w_own = lax.dynamic_slice_in_dim(weight, core * half, half, 0)
    w_oth = lax.dynamic_slice_in_dim(weight, (1 - core) * half, half, 0)
    dims = (((1,), (1,)), ((), ()))
    send = lax.dot_general(full, w_oth, dims, preferred_element_type=jnp.float32)
    got = lax.ppermute(send.astype(jnp.float16), "core", SWAP)
    keep = lax.dot_general(full, w_own, dims, preferred_element_type=jnp.float32)
    keep = lax.optimization_barrier(keep)
    x, z = lax.axis_index("x"), lax.axis_index("zl")
    chips = [2 * lax.rem(x + dx, 4) + (z + dz) % 2 for dx, dz in STEPS]

    def part(j):
        mine = lax.dynamic_slice_in_dim(keep, j * per_chip, per_chip, 0)
        theirs = lax.dynamic_slice_in_dim(got, j * per_chip, per_chip, 0)
        return mine + theirs.astype(jnp.float32)

    parts = [to_chip(part(j).astype(jnp.float16), step) for j, step in zip(chips, STEPS)]
    logits = lax.optimization_barrier(part(chip))
    for v in parts:
        logits = logits + v.astype(jnp.float32)

    block = softmax(jnp.stack([chip, base_own]), logits, ids)
    sources = [2 * lax.rem(x + 4 - dx, 4) + (z + dz) % 2 for dx, dz in STEPS]
    own, st_own = assemble(jnp.stack([chip] + sources), [block] + [to_chip(block, step) for step in STEPS])
    st_oth = lax.ppermute(st_own, "core", SWAP)
    own, st_oth = lax.optimization_barrier((own, st_oth))
    oth = lax.ppermute(own, "core", SWAP)
    everyone = lax.all_to_all(join_stats(st_own, st_oth, 16), PIPE, 0, 0)

    place = jnp.stack([core * half, (1 - core) * half, section * vocab])
    u, picks = products(place, own, oth, ids, weight)

    scales, every_loss = scale_columns(everyone, st_own, st_oth, u)
    hg = scales[:, 0:1] * u[0] + scales[:, 1:2] * u[1] - picks.astype(jnp.float32)
    sent = (hg * 16384.0).astype(jnp.float16).reshape(16, rows, width)
    parts = lax.all_to_all(sent, PIPE, 0, 0)
    hidden_grad = jnp.sum(parts.astype(jnp.float32) * (1.0 / 4096.0), axis=0).astype(jnp.bfloat16)

    losses = lax.dynamic_slice_in_dim(every_loss[0], section * rows, rows, 0)
    weight_grad = weight_gradient(
        jnp.stack([core, base_own, base_oth]), own, oth, gathered, ids, scales, half, width
    )
    return (losses, hidden_grad, weight_grad)


def solution(mesh):
    fine = Mesh(mesh.devices.reshape(4, 4, 4, 2, 2), PIPE + TENSOR)
    return jax.shard_map(
        shards,
        mesh=fine,
        in_specs=(P(PIPE, TENSOR), P(PIPE), P(PIPE, TENSOR)),
        out_specs=(P(PIPE), P(PIPE, TENSOR), P(PIPE, TENSOR)),
        check_vma=False,
    )
```

```python
import functools

import jax
import jax.numpy as jnp
from jax import lax
from jax.experimental import pallas as pl
from jax.experimental.pallas import tpu as pltpu
from jax.sharding import Mesh, PartitionSpec as P

PIPE = ("y", "zh")
CHIPS = ("x", "zl")
TENSOR = ("x", "zl", "core")
SWAP = [(0, 1), (1, 0)]
STEPS = [(1, 0), (3, 0), (0, 1), (2, 1), (2, 0), (1, 1), (3, 1)]
TILE = 512


def join3(v, k):
    return v[3 * k : 3 * k + 1] + v[3 * k + 1 : 3 * k + 2] + v[3 * k + 2 : 3 * k + 3]


def decode(ids):
    ids = ids.astype(jnp.float32).astype(jnp.int32)
    return ids[:, 0:1] * 256 + ids[:, 1:2]


def spread(v, axes, n):
    return lax.all_to_all(jnp.broadcast_to(v[None], (n,) + v.shape), axes, 0, 0)


def to_chip(v, step):
    dx, dz = step
    pairs = [(2 * x + z, 2 * ((x + dx) % 4) + (z ^ dz)) for x in range(4) for z in range(2)]
    return lax.ppermute(v, CHIPS, pairs)


def far(v):
    return pltpu.with_memory_space_constraint(v, pltpu.HBM)


def params(mib):
    return pltpu.CompilerParams(vmem_limit_bytes=mib << 20)


def pack_kernel(targets_ref, hidden_ref, out_ref, targets, sem):
    copy = pltpu.make_async_copy(targets_ref, targets, sem)
    copy.start()
    rows, width = hidden_ref.shape
    copy.wait()
    row = lax.broadcasted_iota(jnp.int32, (rows, 128), 0)
    lane = lax.broadcasted_iota(jnp.int32, (rows, 128), 1)
    ids = jnp.zeros((rows, 128), jnp.int32)
    for r in range(rows):
        t = targets[r]
        high = lax.shift_right_logical(t, 8)
        low = t - high * 256
        ids = jnp.where((row == r) & (lane == 0), high, ids)
        ids = jnp.where((row == r) & (lane == 1), low, ids)
    ids = ids.astype(jnp.float32).astype(jnp.bfloat16)
    out_ref[:, :width] = hidden_ref[...]
    out_ref[:, width:] = ids


def pack(hidden, targets):
    rows, width = hidden.shape
    return pl.pallas_call(
        pack_kernel,
        grid=(1,),
        in_specs=[pl.BlockSpec(memory_space=pltpu.HBM), pl.BlockSpec((rows, width), lambda i: (0, 0))],
        out_specs=pl.BlockSpec((rows, width + 128), lambda i: (0, 0)),
        out_shape=jax.ShapeDtypeStruct((rows, width + 128), jnp.bfloat16),
        scratch_shapes=[pltpu.SMEM((rows,), jnp.int32), pltpu.SemaphoreType.DMA],
        compiler_params=params(4),
    )(far(targets), far(hidden))


def order_kernel(place, *refs):
    rows = refs[0].shape[0]
    for r, block in enumerate(refs[:-1]):
        refs[-1][pl.ds(pl.multiple_of(place[r] * rows, rows), rows)] = block[...]


def around(v, axis):
    rows, width = v.shape
    me = lax.axis_index(axis)
    ring = [lax.ppermute(v, axis, [(i, (i + k) % 4) for i in range(4)]) for k in (1, 3, 2)]
    place = jnp.stack([me] + [lax.rem(me + 4 - k, 4) for k in (1, 3, 2)])
    return pl.pallas_call(
        order_kernel,
        grid_spec=pltpu.PrefetchScalarGridSpec(
            num_scalar_prefetch=1,
            grid=(1,),
            in_specs=[pl.BlockSpec((rows, width), lambda i, s: (0, 0))] * 4,
            out_specs=pl.BlockSpec((4 * rows, width), lambda i, s: (0, 0)),
        ),
        out_shape=jax.ShapeDtypeStruct((4 * rows, width), v.dtype),
        compiler_params=params(8),
    )(place, v, *ring)


def softmax_kernel(place, logits_ref, ids_ref, out_ref):
    rows, half = logits_ref.shape
    logits = logits_ref[...]
    top = jnp.max(logits, axis=1, keepdims=True)
    e = jnp.exp(logits - top)
    s = jnp.sum(e, axis=1, keepdims=True)
    columns = lax.broadcasted_iota(jnp.int32, logits.shape, 1) + place[1]
    pick = jnp.sum(jnp.where(columns == decode(ids_ref[...]), logits, 0.0), axis=1, keepdims=True)
    lane = lax.broadcasted_iota(jnp.int32, (rows, 128), 1)
    stats = jnp.zeros((rows, 128), jnp.float32)
    for k, v in enumerate((top, s, pick)):
        for part in range(3):
            rounded = v.astype(jnp.bfloat16).astype(jnp.float32)
            stats = jnp.where(lane == 3 * k + part, rounded, stats)
            v = v - rounded
    out_ref[:, :half] = e.astype(jnp.bfloat16)
    out_ref[:, half:] = stats.astype(jnp.bfloat16)


def softmax(place, logits, ids):
    rows, half = logits.shape
    return pl.pallas_call(
        softmax_kernel,
        grid_spec=pltpu.PrefetchScalarGridSpec(
            num_scalar_prefetch=1,
            grid=(1,),
            in_specs=[
                pl.BlockSpec((rows, half), lambda i, s: (0, 0)),
                pl.BlockSpec((rows, 128), lambda i, s: (s[0], 0)),
            ],
            out_specs=pl.BlockSpec((rows, half + 128), lambda i, s: (0, 0)),
        ),
        out_shape=jax.ShapeDtypeStruct((rows, half + 128), jnp.bfloat16),
        compiler_params=params(8),
    )(place, logits, ids)


def assemble_kernel(place, *refs):
    blocks, (out_ref, stat_ref) = refs[:-2], refs[-2:]
    rows = blocks[0].shape[0]
    for r, block in enumerate(blocks):
        out_ref[pl.ds(pl.multiple_of(place[r] * rows, rows), rows)] = block[...]
    v = out_ref[:, out_ref.shape[1] - 128 :].astype(jnp.float32).T
    stat_ref[...] = jnp.concatenate([join3(v, 0), join3(v, 1), join3(v, 2), v[16:21]], axis=0)


def assemble(place, blocks):
    rows, width = blocks[0].shape
    tokens = rows * len(blocks)
    return pl.pallas_call(
        assemble_kernel,
        grid_spec=pltpu.PrefetchScalarGridSpec(
            num_scalar_prefetch=1,
            grid=(1,),
            in_specs=[pl.BlockSpec((rows, width), lambda i, s: (0, 0))] * len(blocks),
            out_specs=[
                pl.BlockSpec((tokens, width), lambda i, s: (0, 0)),
                pl.BlockSpec((8, tokens), lambda i, s: (0, 0)),
            ],
        ),
        out_shape=[
            jax.ShapeDtypeStruct((tokens, width), jnp.bfloat16),
            jax.ShapeDtypeStruct((8, tokens), jnp.float32),
        ],
        compiler_params=params(12),
    )(place, *blocks)


def join_kernel(own_ref, oth_ref, out_ref):
    both = jnp.concatenate([own_ref[0:3], oth_ref[0:3], own_ref[6:8]], axis=0)
    for d in range(out_ref.shape[0]):
        out_ref[d] = both


def join_stats(own, oth, copies):
    return pl.pallas_call(
        join_kernel,
        out_shape=jax.ShapeDtypeStruct((copies,) + own.shape, jnp.float32),
        compiler_params=params(4),
    )(own, oth)


def scale_kernel(every_ref, own_ref, oth_ref, u_ref, scale_ref, loss_ref):
    every = every_ref[...]
    upper = jnp.max(jnp.maximum(every[:, 0], every[:, 3]), axis=0, keepdims=True)
    total = jnp.sum(
        every[:, 1] * jnp.exp(every[:, 0] - upper) + every[:, 4] * jnp.exp(every[:, 3] - upper), axis=0, keepdims=True
    )
    picked = jnp.sum(every[:, 2] + every[:, 5], axis=0, keepdims=True)
    loss_ref[...] = upper + jnp.log(total) - picked
    a = jnp.exp(own_ref[0:1] - upper) / total
    b = jnp.exp(oth_ref[0:1] - upper) / total
    scale_ref[...] = jnp.concatenate([a, b, jnp.zeros((126, a.shape[1]), jnp.float32)], axis=0).T


def scale_columns(everyone, own, oth, u):
    tokens = own.shape[1]
    return pl.pallas_call(
        scale_kernel,
        in_specs=[pl.BlockSpec(memory_space=pltpu.VMEM)] * 3 + [pl.BlockSpec(memory_space=pl.ANY)],
        out_shape=[
            jax.ShapeDtypeStruct((tokens, 128), jnp.float32),
            jax.ShapeDtypeStruct((1, tokens), jnp.float32),
        ],
        compiler_params=params(4),
    )(everyone, own, oth, u)


def row_blocks(place, w_ref, held, sems):
    step = held.shape[0] // sems.shape[0]
    copies = []
    for slot in range(sems.shape[0]):
        which, k = divmod(slot, sems.shape[0] // 2)
        source = pl.ds(pl.multiple_of(place[which], step) + k * step, step)
        copies.append(
            pltpu.make_async_copy(w_ref.at[source], held.at[pl.ds(slot * step, step)], sems.at[slot])
        )
    return step, copies


def product_kernel(place, own_ref, ids_ref, oth_ref, w_ref, u_ref, t_ref, held, other, both, sems, sem):
    step, copies = row_blocks(place, w_ref, held, sems)
    fetch = pltpu.make_async_copy(oth_ref, other, sem)
    per_half = len(copies) // 2
    half = step * per_half
    for copy in copies[:per_half]:
        copy.start()
    target = decode(ids_ref[...])
    tokens = target.shape[0]
    t = None
    for which, p_ref in enumerate((own_ref, other)):
        columns = lax.broadcasted_iota(jnp.int32, (tokens, half), 1) + (place[2] + place[which])
        both[tokens:] = jnp.where(columns == target, 1.0, 0.0).astype(jnp.bfloat16)
        if which == 1:
            fetch.wait()
        both[:tokens] = p_ref[:, :half]
        for copy in copies[which * per_half : (which + 1) * per_half]:
            copy.wait()
        if which == 0:
            fetch.start()
            for copy in copies[per_half:]:
                copy.start()
        d = jnp.dot(both[...], held[which * half : (which + 1) * half], preferred_element_type=jnp.float32)
        u_ref[which] = d[:tokens]
        t = d[tokens:] if t is None else t + d[tokens:]
    t_ref[...] = t.astype(jnp.bfloat16)


def products(place, own, oth, ids, weight):
    tokens, width = own.shape[0], weight.shape[1]
    return pl.pallas_call(
        product_kernel,
        grid_spec=pltpu.PrefetchScalarGridSpec(
            num_scalar_prefetch=1,
            grid=(1,),
            in_specs=[
                pl.BlockSpec(memory_space=pltpu.VMEM),
                pl.BlockSpec(memory_space=pltpu.VMEM),
                pl.BlockSpec(memory_space=pltpu.HBM),
                pl.BlockSpec(memory_space=pltpu.HBM),
            ],
            out_specs=[
                pl.BlockSpec((2, tokens, width), lambda i, s: (0, 0, 0)),
                pl.BlockSpec((tokens, width), lambda i, s: (0, 0)),
            ],
            scratch_shapes=[
                pltpu.VMEM(weight.shape, weight.dtype),
                pltpu.VMEM(oth.shape, oth.dtype),
                pltpu.VMEM((2 * tokens, weight.shape[0] // 2), jnp.bfloat16),
                pltpu.SemaphoreType.DMA((4,)),
                pltpu.SemaphoreType.DMA,
            ],
        ),
        out_shape=[
            jax.ShapeDtypeStruct((2, tokens, width), jnp.float32),
            jax.ShapeDtypeStruct((tokens, width), jnp.bfloat16),
        ],
        compiler_params=params(28),
        cost_estimate=pl.CostEstimate(
            flops=4 * tokens * weight.size, bytes_accessed=2 * weight.size, transcendentals=0
        ),
    )(place, own, ids, far(oth), far(weight))


def weight_grad_kernel(steps, place, own_ref, oth_ref, hidden_ref, ids_ref, scale_ref, out_ref):
    i = pl.program_id(0)

    def tile(p_ref, which, j):
        columns = lax.broadcasted_iota(jnp.int32, p_ref.shape, 1) + (place[1 + which] + j * TILE)
        onehot = (columns == decode(ids_ref[...])).astype(jnp.float32)
        scale = scale_ref[:, which : which + 1]
        g = (4.0 * (p_ref[...].astype(jnp.float32) * scale - onehot)).astype(jnp.bfloat16)
        out_ref[...] = lax.dot_general(
            g, hidden_ref[...], (((0,), (0,)), ((), ())), preferred_element_type=jnp.float32
        ).astype(jnp.bfloat16)

    @pl.when(i < steps)
    def _():
        tile(own_ref, 0, i)

    @pl.when(i >= steps)
    def _():
        tile(oth_ref, 1, i - steps)


def weight_gradient(place, own, oth, gathered, ids, scales, half, width):
    tokens = own.shape[0]
    steps = half // TILE
    return pl.pallas_call(
        functools.partial(weight_grad_kernel, steps),
        grid_spec=pltpu.PrefetchScalarGridSpec(
            num_scalar_prefetch=1,
            grid=(2 * steps,),
            in_specs=[
                pl.BlockSpec((tokens, TILE), lambda i, s: (0, jnp.minimum(i, steps - 1))),
                pl.BlockSpec((tokens, TILE), lambda i, s: (0, jnp.maximum(i - steps, 0))),
                pl.BlockSpec((tokens, width), lambda i, s: (0, 0)),
                pl.BlockSpec((tokens, 128), lambda i, s: (0, 0)),
                pl.BlockSpec((tokens, 128), lambda i, s: (0, 0)),
            ],
            out_specs=pl.BlockSpec(
                (TILE, width), lambda i, s: (lax.rem(i + s[0] * steps, 2 * steps), 0)
            ),
        ),
        out_shape=jax.ShapeDtypeStruct((2 * half, width), jnp.bfloat16),
        compiler_params=pltpu.CompilerParams(vmem_limit_bytes=24 << 20),
        cost_estimate=pl.CostEstimate(
            flops=4 * tokens * half * width, bytes_accessed=4 * half * (width + tokens), transcendentals=0
        ),
    )(place, own, far(oth), far(gathered), ids, scales)


def shards(hidden, targets, weight):
    rows, width = hidden.shape
    vocab = weight.shape[0]
    half = vocab // 2
    section = lax.axis_index(PIPE)
    core = lax.axis_index("core")
    chip = lax.axis_index(CHIPS)
    base_own = section * vocab + core * half
    base_oth = section * vocab + (1 - core) * half

    gathered = around(around(pack(hidden, targets), "zh"), "y")
    tokens = gathered.shape[0]
    per_chip = tokens // 8
    full, ids = gathered[:, :width], gathered[:, width:]

    w_own = lax.dynamic_slice_in_dim(weight, core * half, half, 0)
    w_oth = lax.dynamic_slice_in_dim(weight, (1 - core) * half, half, 0)
    dims = (((1,), (1,)), ((), ()))
    send = lax.dot_general(full, w_oth, dims, preferred_element_type=jnp.float32)
    got = lax.ppermute(send.astype(jnp.float16), "core", SWAP)
    keep = lax.dot_general(full, w_own, dims, preferred_element_type=jnp.float32)
    keep = lax.optimization_barrier(keep)
    x, z = lax.axis_index("x"), lax.axis_index("zl")
    chips = [2 * lax.rem(x + dx, 4) + (z + dz) % 2 for dx, dz in STEPS]

    def part(j):
        mine = lax.dynamic_slice_in_dim(keep, j * per_chip, per_chip, 0)
        theirs = lax.dynamic_slice_in_dim(got, j * per_chip, per_chip, 0)
        return mine + theirs.astype(jnp.float32)

    parts = [to_chip(part(j).astype(jnp.float16), step) for j, step in zip(chips, STEPS)]
    logits = lax.optimization_barrier(part(chip))
    for v in parts:
        logits = logits + v.astype(jnp.float32)

    block = softmax(jnp.stack([chip, base_own]), logits, ids)
    sources = [2 * lax.rem(x + 4 - dx, 4) + (z + dz) % 2 for dx, dz in STEPS]
    own, st_own = assemble(jnp.stack([chip] + sources), [block] + [to_chip(block, step) for step in STEPS])
    st_oth = lax.ppermute(st_own, "core", SWAP)
    own, st_oth = lax.optimization_barrier((own, st_oth))
    oth = lax.ppermute(own, "core", SWAP)
    everyone = lax.all_to_all(join_stats(st_own, st_oth, 16), PIPE, 0, 0)

    place = jnp.stack([core * half, (1 - core) * half, section * vocab])
    u, picks = products(place, own, oth, ids, weight)

    scales, every_loss = scale_columns(everyone, st_own, st_oth, u)
    hg = scales[:, 0:1] * u[0] + scales[:, 1:2] * u[1] - picks.astype(jnp.float32)
    sent = (hg * 16384.0).astype(jnp.float16).reshape(16, rows, width)
    parts = lax.all_to_all(sent, PIPE, 0, 0)
    hidden_grad = jnp.sum(parts.astype(jnp.float32) * (1.0 / 4096.0), axis=0).astype(jnp.bfloat16)

    losses = lax.dynamic_slice_in_dim(every_loss[0], section * rows, rows, 0)
    weight_grad = weight_gradient(
        jnp.stack([core, base_own, base_oth]), own, oth, gathered, ids, scales, half, width
    )
    return (losses, hidden_grad, weight_grad)


def solution(mesh):
    fine = Mesh(mesh.devices.reshape(4, 4, 4, 2, 2), PIPE + TENSOR)
    return jax.shard_map(
        shards,
        mesh=fine,
        in_specs=(P(PIPE, TENSOR), P(PIPE), P(PIPE, TENSOR)),
        out_specs=(P(PIPE), P(PIPE, TENSOR), P(PIPE, TENSOR)),
        check_vma=False,
    )
```

```python
import functools

import jax
import jax.numpy as jnp
from jax import lax
from jax.experimental import pallas as pl
from jax.experimental.pallas import tpu as pltpu
from jax.sharding import Mesh, PartitionSpec as P

PIPE = ("y", "zh")
CHIPS = ("x", "zl")
TENSOR = ("x", "zl", "core")
SWAP = [(0, 1), (1, 0)]
STEPS = [(1, 0), (3, 0), (0, 1), (2, 1), (2, 0), (1, 1), (3, 1)]
TILE = 512


def join3(v, k):
    return v[3 * k : 3 * k + 1] + v[3 * k + 1 : 3 * k + 2] + v[3 * k + 2 : 3 * k + 3]


def decode(ids):
    ids = ids.astype(jnp.float32).astype(jnp.int32)
    return ids[:, 0:1] * 256 + ids[:, 1:2]


def spread(v, axes, n):
    return lax.all_to_all(jnp.broadcast_to(v[None], (n,) + v.shape), axes, 0, 0)


def to_chip(v, step):
    dx, dz = step
    pairs = [(2 * x + z, 2 * ((x + dx) % 4) + (z ^ dz)) for x in range(4) for z in range(2)]
    return lax.ppermute(v, CHIPS, pairs)


def far(v):
    return pltpu.with_memory_space_constraint(v, pltpu.HBM)


def params(mib):
    return pltpu.CompilerParams(vmem_limit_bytes=mib << 20)


def pack_kernel(targets_ref, hidden_ref, out_ref, targets, sem):
    copy = pltpu.make_async_copy(targets_ref, targets, sem)
    copy.start()
    rows, width = hidden_ref.shape
    copy.wait()
    row = lax.broadcasted_iota(jnp.int32, (rows, 128), 0)
    lane = lax.broadcasted_iota(jnp.int32, (rows, 128), 1)
    ids = jnp.zeros((rows, 128), jnp.int32)
    for r in range(rows):
        t = targets[r]
        high = lax.shift_right_logical(t, 8)
        low = t - high * 256
        ids = jnp.where((row == r) & (lane == 0), high, ids)
        ids = jnp.where((row == r) & (lane == 1), low, ids)
    ids = ids.astype(jnp.float32).astype(jnp.bfloat16)
    out_ref[:, :width] = hidden_ref[...]
    out_ref[:, width:] = ids


def pack(hidden, targets):
    rows, width = hidden.shape
    return pl.pallas_call(
        pack_kernel,
        grid=(1,),
        in_specs=[pl.BlockSpec(memory_space=pltpu.HBM), pl.BlockSpec((rows, width), lambda i: (0, 0))],
        out_specs=pl.BlockSpec((rows, width + 128), lambda i: (0, 0)),
        out_shape=jax.ShapeDtypeStruct((rows, width + 128), jnp.bfloat16),
        scratch_shapes=[pltpu.SMEM((rows,), jnp.int32), pltpu.SemaphoreType.DMA],
        compiler_params=params(4),
    )(far(targets), far(hidden))


def order_kernel(place, *refs):
    rows = refs[0].shape[0]
    for r, block in enumerate(refs[:-1]):
        refs[-1][pl.ds(pl.multiple_of(place[r] * rows, rows), rows)] = block[...]


def around(v, axis):
    rows, width = v.shape
    me = lax.axis_index(axis)
    ring = [lax.ppermute(v, axis, [(i, (i + k) % 4) for i in range(4)]) for k in (1, 3, 2)]
    place = jnp.stack([me] + [lax.rem(me + 4 - k, 4) for k in (1, 3, 2)])
    return pl.pallas_call(
        order_kernel,
        grid_spec=pltpu.PrefetchScalarGridSpec(
            num_scalar_prefetch=1,
            grid=(1,),
            in_specs=[pl.BlockSpec((rows, width), lambda i, s: (0, 0))] * 4,
            out_specs=pl.BlockSpec((4 * rows, width), lambda i, s: (0, 0)),
        ),
        out_shape=jax.ShapeDtypeStruct((4 * rows, width), v.dtype),
        compiler_params=params(8),
    )(place, v, *ring)


def softmax_kernel(place, logits_ref, ids_ref, out_ref):
    rows, half = logits_ref.shape
    logits = logits_ref[...]
    top = jnp.max(logits, axis=1, keepdims=True)
    e = jnp.exp(logits - top)
    s = jnp.sum(e, axis=1, keepdims=True)
    columns = lax.broadcasted_iota(jnp.int32, logits.shape, 1) + place[1]
    pick = jnp.sum(jnp.where(columns == decode(ids_ref[...]), logits, 0.0), axis=1, keepdims=True)
    lane = lax.broadcasted_iota(jnp.int32, (rows, 128), 1)
    stats = jnp.zeros((rows, 128), jnp.float32)
    for k, v in enumerate((top, s, pick)):
        for part in range(3):
            rounded = v.astype(jnp.bfloat16).astype(jnp.float32)
            stats = jnp.where(lane == 3 * k + part, rounded, stats)
            v = v - rounded
    out_ref[:, :half] = e.astype(jnp.bfloat16)
    out_ref[:, half:] = stats.astype(jnp.bfloat16)


def softmax(place, logits, ids):
    rows, half = logits.shape
    return pl.pallas_call(
        softmax_kernel,
        grid_spec=pltpu.PrefetchScalarGridSpec(
            num_scalar_prefetch=1,
            grid=(1,),
            in_specs=[
                pl.BlockSpec((rows, half), lambda i, s: (0, 0)),
                pl.BlockSpec((rows, 128), lambda i, s: (s[0], 0)),
            ],
            out_specs=pl.BlockSpec((rows, half + 128), lambda i, s: (0, 0)),
        ),
        out_shape=jax.ShapeDtypeStruct((rows, half + 128), jnp.bfloat16),
        compiler_params=params(8),
    )(place, logits, ids)


def assemble_kernel(place, *refs):
    blocks, (out_ref, stat_ref) = refs[:-2], refs[-2:]
    rows = blocks[0].shape[0]
    for r, block in enumerate(blocks):
        out_ref[pl.ds(pl.multiple_of(place[r] * rows, rows), rows)] = block[...]
    v = out_ref[:, out_ref.shape[1] - 128 :].astype(jnp.float32).T
    stat_ref[...] = jnp.concatenate([join3(v, 0), join3(v, 1), join3(v, 2), v[16:21]], axis=0)


def assemble(place, blocks):
    rows, width = blocks[0].shape
    tokens = rows * len(blocks)
    return pl.pallas_call(
        assemble_kernel,
        grid_spec=pltpu.PrefetchScalarGridSpec(
            num_scalar_prefetch=1,
            grid=(1,),
            in_specs=[pl.BlockSpec((rows, width), lambda i, s: (0, 0))] * len(blocks),
            out_specs=[
                pl.BlockSpec((tokens, width), lambda i, s: (0, 0)),
                pl.BlockSpec((8, tokens), lambda i, s: (0, 0)),
            ],
        ),
        out_shape=[
            jax.ShapeDtypeStruct((tokens, width), jnp.bfloat16),
            jax.ShapeDtypeStruct((8, tokens), jnp.float32),
        ],
        compiler_params=params(12),
    )(place, *blocks)


def join_kernel(own_ref, oth_ref, out_ref):
    both = jnp.concatenate([own_ref[0:3], oth_ref[0:3], own_ref[6:8]], axis=0)
    for d in range(out_ref.shape[0]):
        out_ref[d] = both


def join_stats(own, oth, copies):
    return pl.pallas_call(
        join_kernel,
        out_shape=jax.ShapeDtypeStruct((copies,) + own.shape, jnp.float32),
        compiler_params=params(4),
    )(own, oth)


def scale_kernel(every_ref, own_ref, oth_ref, u_ref, scale_ref, loss_ref):
    every = every_ref[...]
    upper = jnp.max(jnp.maximum(every[:, 0], every[:, 3]), axis=0, keepdims=True)
    total = jnp.sum(
        every[:, 1] * jnp.exp(every[:, 0] - upper) + every[:, 4] * jnp.exp(every[:, 3] - upper), axis=0, keepdims=True
    )
    picked = jnp.sum(every[:, 2] + every[:, 5], axis=0, keepdims=True)
    loss_ref[...] = upper + jnp.log(total) - picked
    a = jnp.exp(own_ref[0:1] - upper) / total
    b = jnp.exp(oth_ref[0:1] - upper) / total
    scale_ref[...] = jnp.concatenate([a, b, jnp.zeros((126, a.shape[1]), jnp.float32)], axis=0).T


def scale_columns(everyone, own, oth, u):
    tokens = own.shape[1]
    return pl.pallas_call(
        scale_kernel,
        in_specs=[pl.BlockSpec(memory_space=pltpu.VMEM)] * 3 + [pl.BlockSpec(memory_space=pl.ANY)],
        out_shape=[
            jax.ShapeDtypeStruct((tokens, 128), jnp.float32),
            jax.ShapeDtypeStruct((1, tokens), jnp.float32),
        ],
        compiler_params=params(4),
    )(everyone, own, oth, u)


def row_blocks(place, w_ref, held, sems):
    step = held.shape[0] // sems.shape[0]
    copies = []
    for slot in range(sems.shape[0]):
        which, k = divmod(slot, sems.shape[0] // 2)
        source = pl.ds(pl.multiple_of(place[which], step) + k * step, step)
        copies.append(
            pltpu.make_async_copy(w_ref.at[source], held.at[pl.ds(slot * step, step)], sems.at[slot])
        )
    return step, copies


def product_kernel(place, own_ref, ids_ref, oth_ref, w_ref, u_ref, t_ref, held, other, both, sems, sem):
    step, copies = row_blocks(place, w_ref, held, sems)
    fetch = pltpu.make_async_copy(oth_ref, other, sem)
    per_half = len(copies) // 2
    half = step * per_half
    for copy in copies[:per_half]:
        copy.start()
    target = decode(ids_ref[...])
    tokens = target.shape[0]
    t = None
    for which, p_ref in enumerate((own_ref, other)):
        columns = lax.broadcasted_iota(jnp.int32, (tokens, half), 1) + (place[2] + place[which])
        both[tokens:] = jnp.where(columns == target, 1.0, 0.0).astype(jnp.bfloat16)
        if which == 1:
            fetch.wait()
        both[:tokens] = p_ref[:, :half]
        if which == 0:
            d = None
            for k in range(per_half):
                copies[k].wait()
                if k == 0:
                    fetch.start()
                copies[per_half + k].start()
                part = jnp.dot(
                    both[:, k * step : (k + 1) * step],
                    held[k * step : (k + 1) * step],
                    preferred_element_type=jnp.float32,
                )
                d = part if d is None else d + part
        else:
            for copy in copies[per_half:]:
                copy.wait()
            d = jnp.dot(both[...], held[half:], preferred_element_type=jnp.float32)
        u_ref[which] = d[:tokens]
        t = d[tokens:] if t is None else t + d[tokens:]
    t_ref[...] = t.astype(jnp.bfloat16)


def products(place, own, oth, ids, weight):
    tokens, width = own.shape[0], weight.shape[1]
    return pl.pallas_call(
        product_kernel,
        grid_spec=pltpu.PrefetchScalarGridSpec(
            num_scalar_prefetch=1,
            grid=(1,),
            in_specs=[
                pl.BlockSpec(memory_space=pltpu.VMEM),
                pl.BlockSpec(memory_space=pltpu.VMEM),
                pl.BlockSpec(memory_space=pltpu.HBM),
                pl.BlockSpec(memory_space=pltpu.HBM),
            ],
            out_specs=[
                pl.BlockSpec((2, tokens, width), lambda i, s: (0, 0, 0)),
                pl.BlockSpec((tokens, width), lambda i, s: (0, 0)),
            ],
            scratch_shapes=[
                pltpu.VMEM(weight.shape, weight.dtype),
                pltpu.VMEM(oth.shape, oth.dtype),
                pltpu.VMEM((2 * tokens, weight.shape[0] // 2), jnp.bfloat16),
                pltpu.SemaphoreType.DMA((4,)),
                pltpu.SemaphoreType.DMA,
            ],
        ),
        out_shape=[
            jax.ShapeDtypeStruct((2, tokens, width), jnp.float32),
            jax.ShapeDtypeStruct((tokens, width), jnp.bfloat16),
        ],
        compiler_params=params(28),
        cost_estimate=pl.CostEstimate(
            flops=4 * tokens * weight.size, bytes_accessed=2 * weight.size, transcendentals=0
        ),
    )(place, own, ids, far(oth), far(weight))


def weight_grad_kernel(steps, place, own_ref, oth_ref, hidden_ref, ids_ref, scale_ref, out_ref):
    i = pl.program_id(0)

    def tile(p_ref, which, j):
        columns = lax.broadcasted_iota(jnp.int32, p_ref.shape, 1) + (place[1 + which] + j * TILE)
        onehot = (columns == decode(ids_ref[...])).astype(jnp.float32)
        scale = scale_ref[:, which : which + 1]
        g = (4.0 * (p_ref[...].astype(jnp.float32) * scale - onehot)).astype(jnp.bfloat16)
        out_ref[...] = lax.dot_general(
            g, hidden_ref[...], (((0,), (0,)), ((), ())), preferred_element_type=jnp.float32
        ).astype(jnp.bfloat16)

    @pl.when(i < steps)
    def _():
        tile(own_ref, 0, i)

    @pl.when(i >= steps)
    def _():
        tile(oth_ref, 1, i - steps)


def weight_gradient(place, own, oth, gathered, ids, scales, half, width):
    tokens = own.shape[0]
    steps = half // TILE
    return pl.pallas_call(
        functools.partial(weight_grad_kernel, steps),
        grid_spec=pltpu.PrefetchScalarGridSpec(
            num_scalar_prefetch=1,
            grid=(2 * steps,),
            in_specs=[
                pl.BlockSpec((tokens, TILE), lambda i, s: (0, jnp.minimum(i, steps - 1))),
                pl.BlockSpec((tokens, TILE), lambda i, s: (0, jnp.maximum(i - steps, 0))),
                pl.BlockSpec((tokens, width), lambda i, s: (0, 0)),
                pl.BlockSpec((tokens, 128), lambda i, s: (0, 0)),
                pl.BlockSpec((tokens, 128), lambda i, s: (0, 0)),
            ],
            out_specs=pl.BlockSpec(
                (TILE, width), lambda i, s: (lax.rem(i + s[0] * steps, 2 * steps), 0)
            ),
        ),
        out_shape=jax.ShapeDtypeStruct((2 * half, width), jnp.bfloat16),
        compiler_params=pltpu.CompilerParams(vmem_limit_bytes=24 << 20),
        cost_estimate=pl.CostEstimate(
            flops=4 * tokens * half * width, bytes_accessed=4 * half * (width + tokens), transcendentals=0
        ),
    )(place, own, far(oth), far(gathered), ids, scales)


def shards(hidden, targets, weight):
    rows, width = hidden.shape
    vocab = weight.shape[0]
    half = vocab // 2
    section = lax.axis_index(PIPE)
    core = lax.axis_index("core")
    chip = lax.axis_index(CHIPS)
    base_own = section * vocab + core * half
    base_oth = section * vocab + (1 - core) * half

    gathered = around(around(pack(hidden, targets), "zh"), "y")
    tokens = gathered.shape[0]
    per_chip = tokens // 8
    full, ids = gathered[:, :width], gathered[:, width:]

    w_own = lax.dynamic_slice_in_dim(weight, core * half, half, 0)
    w_oth = lax.dynamic_slice_in_dim(weight, (1 - core) * half, half, 0)
    dims = (((1,), (1,)), ((), ()))
    send = lax.dot_general(full, w_oth, dims, preferred_element_type=jnp.float32)
    got = lax.ppermute(send.astype(jnp.float16), "core", SWAP)
    keep = lax.dot_general(full, w_own, dims, preferred_element_type=jnp.float32)
    keep = lax.optimization_barrier(keep)
    x, z = lax.axis_index("x"), lax.axis_index("zl")
    chips = [2 * lax.rem(x + dx, 4) + (z + dz) % 2 for dx, dz in STEPS]

    def part(j):
        mine = lax.dynamic_slice_in_dim(keep, j * per_chip, per_chip, 0)
        theirs = lax.dynamic_slice_in_dim(got, j * per_chip, per_chip, 0)
        return mine + theirs.astype(jnp.float32)

    parts = [to_chip(part(j).astype(jnp.float16), step) for j, step in zip(chips, STEPS)]
    logits = lax.optimization_barrier(part(chip))
    for v in parts:
        logits = logits + v.astype(jnp.float32)

    block = softmax(jnp.stack([chip, base_own]), logits, ids)
    sources = [2 * lax.rem(x + 4 - dx, 4) + (z + dz) % 2 for dx, dz in STEPS]
    own, st_own = assemble(jnp.stack([chip] + sources), [block] + [to_chip(block, step) for step in STEPS])
    st_oth = lax.ppermute(st_own, "core", SWAP)
    own, st_oth = lax.optimization_barrier((own, st_oth))
    oth = lax.ppermute(own, "core", SWAP)
    everyone = lax.all_to_all(join_stats(st_own, st_oth, 16), PIPE, 0, 0)

    place = jnp.stack([core * half, (1 - core) * half, section * vocab])
    u, picks = products(place, own, oth, ids, weight)

    scales, every_loss = scale_columns(everyone, st_own, st_oth, u)
    hg = scales[:, 0:1] * u[0] + scales[:, 1:2] * u[1] - picks.astype(jnp.float32)
    sent = (hg * 16384.0).astype(jnp.float16).reshape(16, rows, width)
    parts = lax.all_to_all(sent, PIPE, 0, 0)
    hidden_grad = jnp.sum(parts.astype(jnp.float32) * (1.0 / 4096.0), axis=0).astype(jnp.bfloat16)

    losses = lax.dynamic_slice_in_dim(every_loss[0], section * rows, rows, 0)
    weight_grad = weight_gradient(
        jnp.stack([core, base_own, base_oth]), own, oth, gathered, ids, scales, half, width
    )
    return (losses, hidden_grad, weight_grad)


def solution(mesh):
    fine = Mesh(mesh.devices.reshape(4, 4, 4, 2, 2), PIPE + TENSOR)
    return jax.shard_map(
        shards,
        mesh=fine,
        in_specs=(P(PIPE, TENSOR), P(PIPE), P(PIPE, TENSOR)),
        out_specs=(P(PIPE), P(PIPE, TENSOR), P(PIPE, TENSOR)),
        check_vma=False,
    )
```
